1024 devices in a mesh: node: 64 (over z, x), local: 16 (over y, core).
Axes of the slice: x: 8, y: 8, z: 8, core: 2. Of those that a mesh axis runs over, the one named last changes fastest.
Arguments:
- out_grad: bfloat16 [8192, 3584], P(('node', 'local')), may hold values from -6 to 6
- node_ids: int32 [8192, 4], P(('node', 'local')), may hold values from 0 to 63, as said below
- route_weights: bfloat16 [8192, 8], P(('node', 'local')), may hold values from 0.049804688 to 0.59765625
- saved_gate: bfloat16 [32768, 2048], P('node', 'local'), may hold values from -6 to 6
- saved_up: bfloat16 [32768, 2048], P('node', 'local'), may hold values from -6 to 6
- gate_weight: bfloat16 [3584, 131072], P(None, ('node', 'local')), may hold values from -0.1875 to 0.1875
- up_weight: bfloat16 [3584, 131072], P(None, ('node', 'local')), may hold values from -0.1875 to 0.1875
- down_weight: bfloat16 [131072, 3584], P(('node', 'local')), may hold values from -0.09375 to 0.09375
Outputs:
- in_grad: bfloat16 [8192, 3584], P(('node', 'local'))
The draws below stay inside these ranges and needn't reach their ends.
Inputs may be any that keep to these rules, and one draw needn't show every extreme that they name: `node_ids`: each row names 4 different nodes. The 8 tokens of one device name each node at most 1 times in all, some node exactly 1 times; all tokens of the devices that share one index along local name each node exactly 4 * 8 times.
All inputs are finite; a program needn't handle non-finite values.
Results may differ from the reference program's by a relative error of at most 0.024.
Values may be sent and summed in bfloat16 or wider, within the bound.
A program may use at most 32 MiB of HBM per device.

```python
import math
import jax
import jax.numpy as jnp
from jax import lax

D = 3584
FE = 1024
EXP_NODE = 2
TOK_DEV = 8
TOKENS = 8192
EXPERTS = 128
NODE_ROWS = 512
N_NODE = 64
N_LOCAL = 16


def draw_node_ids(key, part):
    key = jax.random.fold_in(key, 5)
    device_total = N_NODE * N_LOCAL
    order_keys = jax.random.split(jax.random.fold_in(key, 11), N_LOCAL)
    node_order = jax.vmap(lambda sub_key: jax.random.permutation(sub_key, N_NODE))(order_keys).astype(jnp.int32)
    token_keys = jax.random.split(jax.random.fold_in(key, 12), device_total)
    token_order = jax.vmap(lambda sub_key: jax.random.permutation(sub_key, TOK_DEV))(token_keys).astype(jnp.int32)
    device = jnp.arange(device_total, dtype=jnp.int32)
    source_node = device // N_LOCAL
    source_local = device % N_LOCAL
    offset = (source_node[:, None, None] + 4 * token_order[:, :, None] + jnp.arange(4, dtype=jnp.int32)[None, None, :]) % N_NODE
    chosen = node_order[source_local[:, None, None], offset]
    return chosen.reshape(device_total * TOK_DEV, 4).astype(jnp.int32)


def shard_levels(rng, extent, pieces, smallest, largest):
    def one(position, shards_of):
        heights = jax.random.uniform(jax.random.fold_in(jax.random.fold_in(rng, 6), position), (shards_of,), jnp.float32, smallest / len(pieces), largest / len(pieces))
        return jnp.repeat(jnp.exp(heights), extent[position] // shards_of).reshape((-1,) + (1,) * (len(extent) - position - 1))

    gain = one(*pieces[0])
    for cut in pieces[1:]:
        gain = gain * one(*cut)
    return gain


def bell_draw(key, dims, scale, reach, shards=(), kind=jnp.bfloat16):
    factor_of = shard_levels(key, dims, shards, -0.22, 0.18) if shards else 1.0
    array = jax.random.normal(key, dims, jnp.float32) * scale * factor_of
    return jnp.minimum(jnp.maximum(array, -reach), reach).astype(kind)


def setup_inputs(seed: int = 0) -> dict:
    arg_keys = jax.random.split(jax.random.key(seed), 9)
    return {
        "out_grad": bell_draw(arg_keys[0], (TOKENS, D), 1.0, 6.0, ((0, 1024),)),
        "node_ids": draw_node_ids(jax.random.fold_in(arg_keys[8], 71), 0),
        "route_weights": jnp.clip(jnp.exp(math.log(0.59765625) - 2.4849066 * jax.random.uniform(arg_keys[2], (TOKENS, 4 * EXP_NODE), jnp.float32) ** shard_levels(arg_keys[2], (TOKENS, 4 * EXP_NODE), ((0, 1024),), -0.2, 0.2)), 0.049804688, 0.59765625).astype(jnp.bfloat16),
        "saved_gate": bell_draw(arg_keys[3], (N_NODE * NODE_ROWS, EXP_NODE * FE), 1.0, 6.0, ((0, 64), (1, 16))),
        "saved_up": bell_draw(arg_keys[4], (N_NODE * NODE_ROWS, EXP_NODE * FE), 1.0, 6.0, ((0, 64), (1, 16))),
        "gate_weight": bell_draw(arg_keys[5], (D, EXPERTS * FE), FE ** -0.5, 0.1875, ((1, 1024),)),
        "up_weight": bell_draw(arg_keys[6], (D, EXPERTS * FE), FE ** -0.5, 0.1875, ((1, 1024),)),
        "down_weight": bell_draw(arg_keys[7], (EXPERTS * FE, D), D ** -0.5, 0.09375, ((0, 1024),)),
    }


def reference(out_grad, node_ids, route_weights, saved_gate, saved_up, gate_weight, up_weight, down_weight):
    pick_count = 4 * TOK_DEV
    node_width = EXP_NODE * FE
    block_width = node_width // N_LOCAL
    ordered = node_ids.reshape(N_NODE, N_LOCAL, pick_count).transpose(1, 0, 2).reshape(N_LOCAL, N_NODE * pick_count)
    onehot = (ordered[:, :, None] == jnp.arange(N_NODE, dtype=jnp.int32)[None, None, :]).astype(jnp.int32)
    earlier = jnp.sum((jnp.cumsum(onehot, axis=1) - onehot) * onehot, axis=2)
    earlier = earlier.reshape(N_LOCAL, N_NODE, pick_count).transpose(1, 0, 2).reshape(TOKENS, 4)
    local_index = ((jnp.arange(TOKENS, dtype=jnp.int32) // TOK_DEV) % N_LOCAL)[:, None]
    row_index = (node_ids * NODE_ROWS + local_index * pick_count + earlier).astype(jnp.int32)
    flat_row = row_index.reshape(-1)
    node_input = jnp.zeros((N_NODE * NODE_ROWS, D), jnp.bfloat16).at[flat_row].set(jnp.repeat(out_grad, 4, axis=0))
    node_gates = jnp.zeros((N_NODE * NODE_ROWS, EXP_NODE), jnp.bfloat16).at[flat_row].set(route_weights.reshape(TOKENS * 4, EXP_NODE))

    def one_node(node_index):
        first_row = (node_index * NODE_ROWS).astype(jnp.int32)
        first_col = (node_index * node_width).astype(jnp.int32)
        node_rows = lax.dynamic_slice_in_dim(node_input, first_row, NODE_ROWS, 0)
        row_gates = lax.dynamic_slice_in_dim(node_gates, first_row, NODE_ROWS, 0).astype(jnp.float32)
        pre_gate = lax.dynamic_slice_in_dim(saved_gate, first_row, NODE_ROWS, 0).astype(jnp.float32)
        pre_up = lax.dynamic_slice_in_dim(saved_up, first_row, NODE_ROWS, 0).astype(jnp.float32)
        w_down = lax.dynamic_slice_in_dim(down_weight, first_col, node_width, 0)
        w_gate = lax.dynamic_slice_in_dim(gate_weight, first_col, node_width, 1)
        w_up = lax.dynamic_slice_in_dim(up_weight, first_col, node_width, 1)
        projected = jnp.dot(node_rows, w_down.T, preferred_element_type=jnp.float32)
        hidden_grad = jnp.repeat(row_gates, FE, axis=1) * projected
        sigma_gate = jax.nn.sigmoid(pre_gate)
        d_gate = (hidden_grad * pre_up * sigma_gate * (1.0 + pre_gate * (1.0 - sigma_gate))).astype(jnp.bfloat16)
        d_up = (hidden_grad * pre_gate * sigma_gate).astype(jnp.bfloat16)
        gate_parts = d_gate.astype(jnp.float32).reshape(NODE_ROWS, N_LOCAL, block_width)
        up_parts = d_up.astype(jnp.float32).reshape(NODE_ROWS, N_LOCAL, block_width)
        gate_cols = w_gate.astype(jnp.float32).reshape(D, N_LOCAL, block_width)
        up_cols = w_up.astype(jnp.float32).reshape(D, N_LOCAL, block_width)
        partial_value = jnp.einsum('rkf,dkf->krd', gate_parts, gate_cols, precision=lax.Precision.HIGHEST)
        partial_value = partial_value + jnp.einsum('rkf,dkf->krd', up_parts, up_cols, precision=lax.Precision.HIGHEST)
        partial_value = lax.optimization_barrier(partial_value.astype(jnp.bfloat16)).astype(jnp.float32)
        return jnp.sum(partial_value, axis=0).astype(jnp.bfloat16)

    node_grad = lax.map(one_node, jnp.arange(N_NODE, dtype=jnp.int32)).reshape(N_NODE * NODE_ROWS, D)
    picked = node_grad[flat_row].astype(jnp.float32).reshape(TOKENS, 4, D)
    return jnp.sum(picked, axis=1).astype(jnp.bfloat16)
```

```python
import functools

import jax
import jax.numpy as jnp
from jax import lax
from jax.experimental import pallas as pl
from jax.experimental.pallas import tpu as pltpu
from jax.sharding import PartitionSpec as P

MESH = pl.DeviceIdType.MESH
F32 = jnp.float32
BF16 = jnp.bfloat16
LANE = 128
SUB = 16
CHUNKS = 2


def iota(shape, dim):
    return lax.broadcasted_iota(jnp.int32, shape, dim)


def one_hot(cond):
    return jnp.where(cond, 1.0, 0.0).astype(BF16)


def dot_nn(a, b):
    return lax.dot_general(a, b, (((1,), (0,)), ((), ())), preferred_element_type=F32)


def dot_nt(a, b):
    return lax.dot_general(a, b, (((1,), (1,)), ((), ())), preferred_element_type=F32)


def kernel(
    cfg,
    og_ref,
    ids_ref,
    rw_ref,
    sg_hbm,
    su_hbm,
    wg_hbm,
    wu_hbm,
    wd_hbm,
    out_ref,
    sg,
    su,
    wd,
    wgu,
    tx,
    rx,
    tx2,
    rx2,
    x0,
    x1,
    pack_t,
    hacc,
    hid,
    part,
    rsib,
    chain_start,
    chain,
    load_sem,
    out_send,
    out_recv,
    back_send,
    back_recv,
    ag_send,
    ag_recv,
    sib_send,
    sib_recv,
    psib_send,
    psib_recv,
    rs_send,
    rs_recv,
):
    nodes, ring, toks, picks, tiles = cfg
    half = ring // 2
    rows = toks * picks
    slots = nodes * SUB
    packed = SUB * rows
    width = tiles * LANE
    xs = (x0, x1)

    node = lax.axis_index("node")
    local = lax.axis_index("local")
    y = local // 2
    core = local % 2
    right = ((y + 1) % ring) * 2 + core
    left = ((y + ring - 1) % ring) * 2 + core
    sibling = y * 2 + (1 - core)

    order = [half]
    for s in range(half - 1, 0, -1):
        order += [s, -s]
    order.append(0)

    def pos(d):
        return order.index(half if d == -half else d)

    streams = ((1, 0, half), (1, 1, half - 1), (-1, 0, half - 1), (-1, 1, half))

    barrier = pltpu.get_barrier_semaphore()

    def greet(i, carry):
        peer = (node + i) % nodes
        pl.semaphore_signal(barrier, inc=1, device_id=(peer, local), device_id_type=MESH)
        return carry

    lax.fori_loop(1, nodes, greet, 0)
    for who in (right, left, sibling):
        pl.semaphore_signal(barrier, inc=1, device_id=(node, who), device_id_type=MESH)

    loads = [
        pltpu.make_async_copy(wd_hbm, wd, load_sem.at[0]),
        pltpu.make_async_copy(sg_hbm, sg, load_sem.at[1]),
        pltpu.make_async_copy(su_hbm, su, load_sem.at[2]),
        pltpu.make_async_copy(wg_hbm, wgu.at[:, pl.ds(0, LANE)], load_sem.at[3]),
        pltpu.make_async_copy(wu_hbm, wgu.at[:, pl.ds(LANE, LANE)], load_sem.at[4]),
    ]
    for load in loads:
        load.start()

    with jax.named_scope("fill_slots"):
        idf = ids_ref[...].astype(F32)
        gates = rw_ref[...].astype(F32)
        lane8 = iota((toks, LANE), 1)
        tok8 = iota((toks, LANE), 0)
        ids_lane = [
            jnp.sum(
                jnp.where(lane8 % toks == tok8, idf[:, j : j + 1], 0.0), axis=0, keepdims=True
            ).astype(jnp.int32)
            for j in range(picks)
        ]
        lane1 = iota((1, LANE), 1)
        slot_row = iota((slots, LANE), 0)
        hit = None
        for j in range(picks):
            key = ids_lane[j] * SUB + lane1 // toks
            same = slot_row == key
            hit = same if hit is None else hit | same
        spread = one_hot(hit)
        pick_key = jnp.full((1, LANE), -1, jnp.int32)
        for j in range(picks):
            mine = ((lane1 // toks) % picks == j) & (lane1 < 2 * rows)
            pick_key = jnp.where(mine, ids_lane[j] * SUB + (SUB - 2) + lane1 // rows, pick_key)
        spread_meta = one_hot(slot_row == pick_key)
        meta = [
            jnp.where(
                lane8 < LANE // 2,
                gates[:, 2 * j : 2 * j + 1],
                gates[:, 2 * j + 1 : 2 * j + 2],
            )
            for j in range(picks)
        ]
        meta = jnp.concatenate(
            meta + [jnp.ones((rows, LANE), F32), jnp.zeros((LANE - 2 * rows, LANE), F32)], axis=0
        ).astype(BF16)
        meta_slots = dot_nn(spread_meta, meta)
        grads = og_ref[...].astype(F32)
        for c in range(CHUNKS):
            stack = [
                grads[:, c * width + k * LANE : c * width + (k + 1) * LANE] for k in range(tiles)
            ]
            stack.append(jnp.zeros((LANE - tiles * toks, LANE), F32))
            block = dot_nn(spread, jnp.concatenate(stack, axis=0).astype(BF16))
            if c == 0:
                block = block + meta_slots
            tx[c] = block.astype(BF16).reshape(nodes, SUB, LANE)
            rx[c, node] = tx[c, node]

    pl.semaphore_wait(barrier, nodes - 1 + 3)

    def to_node(src, dst, send_sem, recv_sem, c):
        def go(i, carry):
            peer = (node + i) % nodes
            pltpu.make_async_remote_copy(
                src_ref=src.at[c, peer],
                dst_ref=dst.at[c, node],
                send_sem=send_sem.at[c],
                recv_sem=recv_sem.at[c],
                device_id=(peer, local),
                device_id_type=MESH,
            ).start()
            return carry

        lax.fori_loop(1, nodes, go, 0)

    def all_of(src, dst, send_sem, recv_sem, c):
        return pltpu.make_async_remote_copy(
            src_ref=src.at[c, pl.ds(0, nodes - 1)],
            dst_ref=dst.at[c, pl.ds(0, nodes - 1)],
            send_sem=send_sem.at[c],
            recv_sem=recv_sem.at[c],
            device_id=(node, sibling),
            device_id_type=MESH,
        )

    for c in range(CHUNKS):
        to_node(tx, rx, out_send, out_recv, c)

    def ag(c, st, s):
        way, h, _ = streams[st]
        return pltpu.make_async_remote_copy(
            src_ref=xs[c].at[pos(-way * (s - 1)), 0, h],
            dst_ref=xs[c].at[pos(-way * s), 0, h],
            send_sem=ag_send.at[c, st, s - 1],
            recv_sem=ag_recv.at[c, st, s - 1],
            device_id=(node, right if way > 0 else left),
            device_id_type=MESH,
        )

    def to_sibling(c, p, h):
        return pltpu.make_async_remote_copy(
            src_ref=xs[c].at[p, 0, h],
            dst_ref=xs[c].at[p, 1, h],
            send_sem=sib_send.at[c, p, h],
            recv_sem=sib_recv.at[c, p, h],
            device_id=(node, sibling),
            device_id_type=MESH,
        )

    def ag_start(c):
        for st in range(4):
            if streams[st][2] > 0:
                ag(c, st, 1).start()
        for h in range(2):
            to_sibling(c, pos(0), h).start()

    def ag_step(c, s):
        for st in (0, 3, 1, 2):
            way, h, hops = streams[st]
            if s <= hops:
                ag(c, st, s).wait_recv()
                if s < hops:
                    ag(c, st, s + 1).start()
                to_sibling(c, pos(-way * s), h).start()

    def sib_wait(c, ps):
        for p in ps:
            for h in range(2):
                to_sibling(c, p, h).wait_recv()

    def fill_key():
        flat = rx[0].reshape(slots, LANE)
        first = one_hot(iota((SUB, LANE), 1) == 0)
        lane_s = iota((SUB, slots), 1)
        flag = jnp.where(lane_s % SUB == SUB - 1, dot_nt(first, flat), 0.0).astype(BF16)
        owner = one_hot(iota((slots, LANE), 0) // SUB == iota((slots, LANE), 1))
        by_node = dot_nn(flag, owner).astype(BF16)
        below = one_hot(iota((LANE, slots), 0) <= iota((LANE, slots), 1) // SUB)
        equal = one_hot(iota((LANE, slots), 0) == iota((LANE, slots), 1) // SUB)
        count = dot_nn(by_node, below)[0:1]
        filled = dot_nn(by_node, equal)[0:1]
        lane = iota((1, slots), 1)
        key = (lane % SUB) * rows + count.astype(jnp.int32) - 1
        return jnp.where(filled > 0.5, key, -1)

    def fill_key_rows():
        flat = rx[0].reshape(slots, LANE)
        take = one_hot(iota((LANE, slots), 1) == iota((LANE, slots), 0) * SUB + SUB - 1)
        by_node = dot_nn(take, flat).astype(BF16)
        below = one_hot(iota((slots, LANE), 1) <= iota((slots, LANE), 0) // SUB)
        equal = one_hot(iota((slots, LANE), 1) == iota((slots, LANE), 0) // SUB)
        count = dot_nn(below, by_node)
        filled = dot_nn(equal, by_node)
        key = (iota((slots, LANE), 0) % SUB) * rows + count.astype(jnp.int32) - 1
        return jnp.where(filled > 0.5, key, -1)

    def compact(c, pack):
        got = dot_nn(pack, rx[c].reshape(slots, LANE)).astype(BF16)
        for k in range(tiles + (1 if c == 0 else 0)):
            src = k if k < tiles else SUB - 2
            xs[c][pos(0), 0, :, :, k * LANE : (k + 1) * LANE] = got[
                src * rows : (src + 1) * rows
            ].reshape(2, rows // 2, LANE)

    def project(c, p0, p1):
        lhs = xs[c][p0:p1, :, :, :, 0:width].reshape((p1 - p0) * 2 * rows, width)
        value = dot_nt(lhs, wd[:, c * width : (c + 1) * width])
        span = pl.ds(p0 * 2 * rows, (p1 - p0) * 2 * rows)
        if c == 0:
            hacc[span, :] = value
        else:
            hacc[span, :] = hacc[span, :] + value

    own_slot = local // (ring * 2 // 2)

    def activate(p0, p1):
        for p in range(p0, p1):
            for who in range(2):
                src_core = core if who == 0 else 1 - core
                src = ((y + order[p] + ring) % ring) * 2 + src_core
                a = sg[src].astype(F32)
                b = su[src].astype(F32)
                g = xs[0][p, who, :, :, width : width + LANE].reshape(rows, LANE).astype(F32)
                gate = jnp.where(own_slot == 0, g[:, 0:1], g[:, LANE // 2 : LANE // 2 + 1])
                base = (p * 2 + who) * rows
                grad = gate * hacc[base : base + rows, :]
                sig = 1.0 / (1.0 + jnp.exp(-a))
                hid[p, who, :, 0:LANE] = (grad * b * sig * (1.0 + a * (1.0 - sig))).astype(BF16)
                hid[p, who, :, LANE : 2 * LANE] = (grad * a * sig).astype(BF16)

    def psib(c, p):
        return pltpu.make_async_remote_copy(
            src_ref=part.at[c, p, 1],
            dst_ref=rsib.at[c, p],
            send_sem=psib_send.at[c, p],
            recv_sem=psib_recv.at[c, p],
            device_id=(node, sibling),
            device_id_type=MESH,
        )

    step_cols = 2 * LANE if width % (2 * LANE) == 0 else LANE

    def expand(c, p0, p1):
        lhs = hid[p0:p1].reshape((p1 - p0) * 2 * rows, 2 * LANE)
        for n in range(0, width, step_cols):
            value = dot_nt(lhs, wgu[c * width + n : c * width + n + step_cols, :])
            part[c, p0:p1, :, :, :, n : n + step_cols] = value.astype(BF16).reshape(
                p1 - p0, 2, 2, rows // 2, step_cols
            )
        for p in range(p0, p1):
            psib(c, p).start()

    def chip_sum(c, p, h):
        return part[c, p, 0, h].astype(F32) + rsib[c, p, h].astype(F32)

    def rs(c, st, s):
        way = streams[st][0]
        return pltpu.make_async_remote_copy(
            src_ref=chain_start.at[c, st] if s == 1 else chain.at[c, st, s - 2],
            dst_ref=chain.at[c, st, s - 1],
            send_sem=rs_send.at[c, st, s - 1],
            recv_sem=rs_recv.at[c, st, s - 1],
            device_id=(node, right if way > 0 else left),
            device_id_type=MESH,
        )

    def rs_start(c):
        for p in range(3):
            psib(c, p).wait_recv()
        for st in (0, 3, 1, 2):
            way, h, hops = streams[st]
            chain_start[c, st] = chip_sum(c, pos(way * hops), h).astype(BF16)
            rs(c, st, 1).start()

    def rs_step(c, s):
        for st in (0, 3, 1, 2):
            way, h, hops = streams[st]
            if s < hops:
                rs(c, st, s).wait_recv()
                total = chain[c, st, s - 1].astype(F32) + chip_sum(c, pos(way * (hops - s)), h)
                chain[c, st, s - 1] = total.astype(BF16)
                rs(c, st, s + 1).start()

    def rs_finish(c):
        sums = []
        for h in range(2):
            total = chip_sum(c, pos(0), h)
            for st in range(4):
                way, sh, hops = streams[st]
                if sh == h:
                    rs(c, st, hops).wait_recv()
                    total = total + chain[c, st, hops - 1].astype(F32)
            sums.append(total)
        total = jnp.concatenate(sums, axis=0).astype(BF16)
        stack = [total[:, k * LANE : (k + 1) * LANE] for k in range(tiles)]
        stack.append(jnp.zeros(((SUB - tiles) * rows, LANE), BF16))
        back = dot_nn(pack_t[...], jnp.concatenate(stack, axis=0))
        tx2[c] = back.astype(BF16).reshape(nodes, SUB, LANE)
        rx2[c, node] = tx2[c, node]
        to_node(tx2, rx2, back_send, back_recv, c)

    def combine(c, merge):
        all_of(tx2, rx2, back_send, back_recv, c).wait_recv()
        got = dot_nn(merge, rx2[c].reshape(slots, LANE))
        for k in range(tiles):
            out_ref[:, c * width + k * LANE : c * width + (k + 1) * LANE] = got[
                k * toks : (k + 1) * toks
            ].astype(BF16)

    all_of(tx, rx, out_send, out_recv, 0).wait_recv()
    with jax.named_scope("compact"):
        key = fill_key()
        pack = one_hot(iota((packed, slots), 0) == key)
        compact(0, pack)
    ag_start(0)
    with jax.named_scope("unpack_matrix"):
        key_rows = fill_key_rows()
        for q in range(packed // LANE):
            pack_t[:, q * LANE : (q + 1) * LANE] = one_hot(
                key_rows == iota((slots, LANE), 1) + q * LANE
            )
    for load in loads:
        load.wait()
    ag_step(0, 1)
    all_of(tx, rx, out_send, out_recv, 1).wait_recv()
    with jax.named_scope("compact"):
        compact(1, pack)
    ag_start(1)
    last = len(order) - 1

    def pair(s):
        return (0, 1) if s == half else (pos(s), pos(-s) + 1) if s else (last, last + 1)

    for s in range(1, half + 1):
        if s < half:
            ag_step(0, s + 1)
        ag_step(1, s)
        p0, p1 = pair(s - 1)
        for c in range(CHUNKS):
            sib_wait(c, range(p0, p1))
            project(c, p0, p1)
        activate(p0, p1)
    p0, p1 = pair(half)
    for c in range(CHUNKS):
        sib_wait(c, range(p0, p1))
        project(c, p0, p1)
    activate(p0, p1)

    expand(0, 0, 3)
    rs_start(0)
    expand(1, 0, 3)
    rs_start(1)
    expand(0, 3, last + 1)
    for p in range(3, last + 1):
        psib(0, p).wait_recv()
    rs_step(0, 1)
    expand(1, 3, last + 1)
    for p in range(3, last + 1):
        psib(1, p).wait_recv()
    rs_step(1, 1)
    for s in range(2, half):
        for c in range(CHUNKS):
            rs_step(c, s)
    for c in range(CHUNKS):
        rs_finish(c)
    with jax.named_scope("merge_matrix"):
        spot = iota((LANE, nodes * SUB), 1)
        tok_row = one_hot(iota((LANE, toks), 0) % toks == iota((LANE, toks), 1))
        ids_rows = dot_nn(tok_row, idf.astype(BF16)).astype(jnp.int32)
        row_tile = iota((LANE, 1), 0) // toks
        hit = None
        for j in range(picks):
            same = spot == ids_rows[:, j : j + 1] * SUB + row_tile
            hit = same if hit is None else hit | same
        merge = one_hot(hit)
    for c in range(CHUNKS):
        combine(c, merge)

    for c in range(CHUNKS):
        all_of(tx, rx, out_send, out_recv, c).wait_send()
        all_of(tx2, rx2, back_send, back_recv, c).wait_send()
        for st in range(4):
            for s in range(1, streams[st][2] + 1):
                ag(c, st, s).wait_send()
                rs(c, st, s).wait_send()
        for p in range(last + 1):
            for h in range(2):
                to_sibling(c, p, h).wait_send()
            psib(c, p).wait_send()


def layer(cfg, og, ids, rw, sg, su, wg, wu, wd):
    nodes, ring, toks, picks, tiles = cfg
    half = ring // 2
    rows = toks * picks
    width = tiles * LANE
    slots = nodes * SUB
    piece = rows // 2
    dma = pltpu.SemaphoreType.DMA
    sg = sg.reshape(2 * ring, rows, LANE)
    su = su.reshape(2 * ring, rows, LANE)
    in_vmem = pl.BlockSpec(memory_space=pltpu.VMEM)
    anywhere = pl.BlockSpec(memory_space=pl.ANY)
    return pl.pallas_call(
        functools.partial(kernel, cfg),
        out_shape=jax.ShapeDtypeStruct(og.shape, BF16),
        in_specs=[in_vmem] * 3 + [anywhere] * 5,
        out_specs=in_vmem,
        scratch_shapes=[
            pltpu.VMEM(sg.shape, BF16),
            pltpu.VMEM(su.shape, BF16),
            pltpu.VMEM(wd.shape, BF16),
            pltpu.VMEM((wg.shape[0], 2 * LANE), BF16),
            pltpu.VMEM((CHUNKS, nodes, SUB, LANE), BF16),
            pltpu.VMEM((CHUNKS, nodes, SUB, LANE), BF16),
            pltpu.VMEM((CHUNKS, nodes, SUB, LANE), BF16),
            pltpu.VMEM((CHUNKS, nodes, SUB, LANE), BF16),
            pltpu.VMEM((ring, 2, 2, piece, width + LANE), BF16),
            pltpu.VMEM((ring, 2, 2, piece, width), BF16),
            pltpu.VMEM((slots, SUB * rows), BF16),
            pltpu.VMEM((ring * 2 * rows, LANE), F32),
            pltpu.VMEM((ring, 2, rows, 2 * LANE), BF16),
            pltpu.VMEM((CHUNKS, ring, 2, 2, piece, width), BF16),
            pltpu.VMEM((CHUNKS, ring, 2, piece, width), BF16),
            pltpu.VMEM((CHUNKS, 4, piece, width), BF16),
            pltpu.VMEM((CHUNKS, 4, half, piece, width), BF16),
            dma((5,)),
            dma((CHUNKS,)),
            dma((CHUNKS,)),
            dma((CHUNKS,)),
            dma((CHUNKS,)),
            dma((CHUNKS, 4, half)),
            dma((CHUNKS, 4, half)),
            dma((CHUNKS, ring, 2)),
            dma((CHUNKS, ring, 2)),
            dma((CHUNKS, ring)),
            dma((CHUNKS, ring)),
            dma((CHUNKS, 4, half)),
            dma((CHUNKS, 4, half)),
        ],
        compiler_params=pltpu.CompilerParams(
            collective_id=0, has_side_effects=True, vmem_limit_bytes=48 * 1024 * 1024
        ),
    )(og, ids, rw, sg, su, wg, wu, wd)


def solution(mesh):
    nodes = mesh.shape["node"]
    ring = mesh.shape["local"] // 2

    def shards(og, ids, rw, sg, su, wg, wu, wd):
        toks, model = og.shape
        cfg = (nodes, ring, toks, ids.shape[1], model // (CHUNKS * LANE))
        return layer(cfg, og, ids, rw, sg, su, wg, wu, wd)

    return jax.shard_map(
        shards,
        mesh=mesh,
        in_specs=(
            P(("node", "local"), None),
            P(("node", "local"), None),
            P(("node", "local"), None),
            P("node", "local"),
            P("node", "local"),
            P(None, ("node", "local")),
            P(None, ("node", "local")),
            P(("node", "local"), None),
        ),
        out_specs=P(("node", "local"), None),
        check_vma=False,
    )
```

```python
import functools
import math

import jax
import jax.numpy as jnp
from jax import lax
from jax.experimental import pallas as pl
from jax.experimental.pallas import tpu as pltpu
from jax.sharding import PartitionSpec as P

MESH = pl.DeviceIdType.MESH
F32 = jnp.float32
BF16 = jnp.bfloat16
LANE = 128
SUB = 16
CHUNKS = 2
PARTS = 1
C1_AFTER = 0
RS_LAG = 2
VMEM_BYTES = 63 * 1024 * 1024


def iota(shape, dim):
    return lax.broadcasted_iota(jnp.int32, shape, dim)


def one_hot(cond):
    return jnp.where(cond, 1.0, 0.0).astype(BF16)


def dot_nn(a, b):
    return lax.dot_general(a, b, (((1,), (0,)), ((), ())), preferred_element_type=F32)


def dot_nt(a, b):
    return lax.dot_general(a, b, (((1,), (1,)), ((), ())), preferred_element_type=F32)


def kernel(
    cfg,
    og_hbm,
    ids_hbm,
    rw_hbm,
    sg_hbm,
    su_hbm,
    wg_hbm,
    wu_hbm,
    wd_hbm,
    out_ref,
    og_ref,
    ids_ref,
    rw_ref,
    sg,
    su,
    wd,
    wgu,
    tx,
    rx,
    tx2,
    rx2,
    x0,
    x1,
    pack_t,
    hacc,
    hid,
    part,
    rsib,
    chain_start,
    chain,
    load_sem,
    out_send,
    out_recv,
    back_send,
    back_recv,
    ag_send,
    ag_recv,
    sib_send,
    sib_recv,
    psib_send,
    psib_recv,
    rs_send,
    rs_recv,
):
    nodes, ring, toks, picks, tiles = cfg
    half = ring // 2
    rows = toks * picks
    slots = nodes * SUB
    packed = SUB * rows
    width = tiles * LANE
    xs = (x0, x1)

    node = lax.axis_index("node")
    local = lax.axis_index("local")
    y = local // 2
    core = local % 2
    right = ((y + 1) % ring) * 2 + core
    left = ((y + ring - 1) % ring) * 2 + core
    sibling = y * 2 + (1 - core)

    order = [half]
    for s in range(half - 1, 0, -1):
        order += [s, -s]
    order.append(0)

    def pos(d):
        return order.index(half if d == -half else d)

    streams = ((1, 0, half), (1, 1, half - 1), (-1, 0, half - 1), (-1, 1, half))

    firsts = [
        pltpu.make_async_copy(ids_hbm, ids_ref, load_sem.at[5]),
        pltpu.make_async_copy(rw_hbm, rw_ref, load_sem.at[6]),
        pltpu.make_async_copy(og_hbm, og_ref, load_sem.at[7]),
    ]
    for first in firsts:
        first.start()

    barrier = pltpu.get_barrier_semaphore()

    side = math.isqrt(nodes)

    def farthest(j):
        return side // 2 + ((j + 1) // 2) * (1 - 2 * (j % 2))

    def peer_at(i):
        first = (node // side + farthest(i // side) + side) % side
        second = (node % side + farthest(i % side) + side) % side
        return first * side + second

    def greet(i, carry):
        peer = peer_at(i)
        pl.semaphore_signal(barrier, inc=1, device_id=(peer, local), device_id_type=MESH)
        return carry

    lax.fori_loop(0, nodes - 1, greet, 0)
    for who in (right, left, sibling):
        pl.semaphore_signal(barrier, inc=1, device_id=(node, who), device_id_type=MESH)

    loads = [
        pltpu.make_async_copy(wd_hbm, wd, load_sem.at[0]),
        pltpu.make_async_copy(sg_hbm, sg, load_sem.at[1]),
        pltpu.make_async_copy(su_hbm, su, load_sem.at[2]),
        pltpu.make_async_copy(wg_hbm, wgu.at[:, pl.ds(0, LANE)], load_sem.at[3]),
        pltpu.make_async_copy(wu_hbm, wgu.at[:, pl.ds(LANE, LANE)], load_sem.at[4]),
    ]
    for load in loads:
        load.start()

    for first in firsts:
        first.wait()
    with jax.named_scope("fill_slots"):
        idf = ids_ref[...].astype(F32).astype(BF16)
        gates = rw_ref[...].astype(F32)
        lane8 = iota((toks, LANE), 1)
        repeat = one_hot(lane8 % toks == iota((toks, LANE), 0))
        ids_lanes = dot_nn(idf, repeat).astype(jnp.int32)
        ids_lane = [ids_lanes[j : j + 1] for j in range(picks)]
        lane1 = iota((1, LANE), 1)
        slot_row = iota((slots, LANE), 0)
        hit = None
        for j in range(picks):
            key = ids_lane[j] * SUB + lane1 // toks
            same = slot_row == key
            hit = same if hit is None else hit | same
        spread = one_hot(hit)
        pick_key = jnp.full((1, LANE), -1, jnp.int32)
        for j in range(picks):
            mine = ((lane1 // toks) % picks == j) & (lane1 < 2 * rows)
            pick_key = jnp.where(mine, ids_lane[j] * SUB + (SUB - 2) + lane1 // rows, pick_key)
        spread_meta = one_hot(slot_row == pick_key)
        meta = [
            jnp.where(
                lane8 < LANE // 2,
                gates[:, 2 * j : 2 * j + 1],
                gates[:, 2 * j + 1 : 2 * j + 2],
            )
            for j in range(picks)
        ]
        meta = jnp.concatenate(
            meta + [jnp.ones((rows, LANE), F32), jnp.zeros((LANE - 2 * rows, LANE), F32)], axis=0
        ).astype(BF16)
        meta_slots = dot_nn(spread_meta, meta)
        grads = og_ref[...].astype(F32)
        for c in range(CHUNKS):
            stack = [
                grads[:, c * width + k * LANE : c * width + (k + 1) * LANE] for k in range(tiles)
            ]
            stack.append(jnp.zeros((LANE - tiles * toks, LANE), F32))
            block = dot_nn(spread, jnp.concatenate(stack, axis=0).astype(BF16))
            if c == 0:
                block = block + meta_slots
            tx[c] = block.astype(BF16).reshape(nodes, SUB, LANE)
            rx[c, node] = tx[c, node]

    pl.semaphore_wait(barrier, nodes - 1 + 3)

    def to_node(src, dst, send_sem, recv_sem, c, lo=0, hi=nodes - 1):
        def go(i, carry):
            peer = peer_at(i)
            pltpu.make_async_remote_copy(
                src_ref=src.at[c, peer],
                dst_ref=dst.at[c, node],
                send_sem=send_sem.at[c],
                recv_sem=recv_sem.at[c],
                device_id=(peer, local),
                device_id_type=MESH,
            ).start()
            return carry

        lax.fori_loop(lo, hi, go, 0)

    def all_of(src, dst, send_sem, recv_sem, c):
        return pltpu.make_async_remote_copy(
            src_ref=src.at[c, pl.ds(0, nodes - 1)],
            dst_ref=dst.at[c, pl.ds(0, nodes - 1)],
            send_sem=send_sem.at[c],
            recv_sem=recv_sem.at[c],
            device_id=(node, sibling),
            device_id_type=MESH,
        )

    to_node(tx, rx, out_send, out_recv, 0)
    to_node(tx, rx, out_send, out_recv, 1)

    def cols(c, q):
        lo = q * (tiles // PARTS) * LANE
        hi = (q + 1) * (tiles // PARTS) * LANE
        if q == PARTS - 1:
            hi = width + (LANE if c == 0 else 0)
        return pl.ds(lo, hi - lo)

    def ag(c, st, s, q):
        way, h, _ = streams[st]
        return pltpu.make_async_remote_copy(
            src_ref=xs[c].at[pos(-way * (s - 1)), 0, h, :, cols(c, q)],
            dst_ref=xs[c].at[pos(-way * s), 0, h, :, cols(c, q)],
            send_sem=ag_send.at[c, st, s - 1, q],
            recv_sem=ag_recv.at[c, st, s - 1, q],
            device_id=(node, right if way > 0 else left),
            device_id_type=MESH,
        )

    def to_sibling(c, p):
        return pltpu.make_async_remote_copy(
            src_ref=xs[c].at[p, 0],
            dst_ref=xs[c].at[p, 1],
            send_sem=sib_send.at[c, p],
            recv_sem=sib_recv.at[c, p],
            device_id=(node, sibling),
            device_id_type=MESH,
        )

    turns = (0, 3, 1, 2)

    def ag_start(c):
        for q in range(PARTS):
            for st in turns:
                ag(c, st, 1, q).start()
        to_sibling(c, pos(0)).start()

    def ag_step(c, s):
        for q in range(PARTS):
            for st in turns:
                way, h, hops = streams[st]
                if s <= hops:
                    ag(c, st, s, q).wait_recv()
                    if s < hops:
                        ag(c, st, s + 1, q).start()

        for p in sorted({pos(s), pos(-s)}):
            to_sibling(c, p).start()

    def sib_wait(c, ps):
        for p in ps:
            to_sibling(c, p).wait_recv()

    def key_constants():
        first = one_hot(iota((SUB, LANE), 1) == 0)
        owner = one_hot(iota((slots, LANE), 0) // SUB == iota((slots, LANE), 1))
        below = one_hot(iota((LANE, slots), 0) <= iota((LANE, slots), 1) // SUB)
        equal = one_hot(iota((LANE, slots), 0) == iota((LANE, slots), 1) // SUB)
        return first, owner, below, equal

    def fill_key(constants):
        first, owner, below, equal = constants
        flat = rx[0].reshape(slots, LANE)
        lane_s = iota((SUB, slots), 1)
        flag = jnp.where(lane_s % SUB == SUB - 1, dot_nt(first, flat), 0.0).astype(BF16)
        by_node = dot_nn(flag, owner).astype(BF16)
        count = dot_nn(by_node, below)[0:1]
        filled = dot_nn(by_node, equal)[0:1]
        lane = iota((1, slots), 1)
        key = (lane % SUB) * rows + count.astype(jnp.int32) - 1
        return jnp.where(filled > 0.5, key, -1)

    def fill_key_rows():
        flat = rx[0].reshape(slots, LANE)
        take = one_hot(iota((LANE, slots), 1) == iota((LANE, slots), 0) * SUB + SUB - 1)
        by_node = dot_nn(take, flat).astype(BF16)
        below = one_hot(iota((slots, LANE), 1) <= iota((slots, LANE), 0) // SUB)
        equal = one_hot(iota((slots, LANE), 1) == iota((slots, LANE), 0) // SUB)
        count = dot_nn(below, by_node)
        filled = dot_nn(equal, by_node)
        key = (iota((slots, LANE), 0) % SUB) * rows + count.astype(jnp.int32) - 1
        return jnp.where(filled > 0.5, key, -1)

    def compact(c, pack):
        got = dot_nn(pack, rx[c].reshape(slots, LANE)).astype(BF16)
        for k in range(tiles + (1 if c == 0 else 0)):
            src = k if k < tiles else SUB - 2
            xs[c][pos(0), 0, :, :, k * LANE : (k + 1) * LANE] = got[
                src * rows : (src + 1) * rows
            ].reshape(2, rows // 2, LANE)

    def project(c, p0, p1):
        lhs = xs[c][p0:p1, :, :, :, 0:width].reshape((p1 - p0) * 2 * rows, width)
        value = dot_nt(lhs, wd[:, c * width : (c + 1) * width])
        span = pl.ds(p0 * 2 * rows, (p1 - p0) * 2 * rows)
        if c == 0:
            hacc[span, :] = value
        else:
            hacc[span, :] = hacc[span, :] + value

    own_slot = local // (ring * 2 // 2)

    def activate(p0, p1):
        for p in range(p0, p1):
            for who in range(2):
                src_core = core if who == 0 else 1 - core
                src = ((y + order[p] + ring) % ring) * 2 + src_core
                a = sg[src].astype(F32)
                b = su[src].astype(F32)
                g = xs[0][p, who, :, :, width : width + LANE].reshape(rows, LANE).astype(F32)
                gate = jnp.where(own_slot == 0, g[:, 0:1], g[:, LANE // 2 : LANE // 2 + 1])
                base = (p * 2 + who) * rows
                grad = gate * hacc[base : base + rows, :]
                sig = 1.0 / (1.0 + jnp.exp(-a))
                hid[p, who, :, 0:LANE] = (grad * b * sig * (1.0 + a * (1.0 - sig))).astype(BF16)
                hid[p, who, :, LANE : 2 * LANE] = (grad * a * sig).astype(BF16)

    def psib(c, p):
        return pltpu.make_async_remote_copy(
            src_ref=part.at[c, p, 1],
            dst_ref=rsib.at[c, p],
            send_sem=psib_send.at[c, p],
            recv_sem=psib_recv.at[c, p],
            device_id=(node, sibling),
            device_id_type=MESH,
        )

    step_cols = 2 * LANE if width % (2 * LANE) == 0 else LANE

    def expand(c, p0, p1):
        lhs = hid[p0:p1].reshape((p1 - p0) * 2 * rows, 2 * LANE)
        for n in range(0, width, step_cols):
            value = dot_nt(lhs, wgu[c * width + n : c * width + n + step_cols, :])
            part[c, p0:p1, :, :, :, n : n + step_cols] = value.astype(BF16).reshape(
                p1 - p0, 2, 2, rows // 2, step_cols
            )
        for p in range(p0, p1):
            psib(c, p).start()

    def chip_sum(c, p, h):
        return part[c, p, 0, h].astype(F32) + rsib[c, p, h].astype(F32)

    def part_cols(q):
        return pl.ds(q * (width // PARTS), width // PARTS)

    def rs(c, st, s, q):
        way = streams[st][0]
        src = chain_start.at[c, st] if s == 1 else chain.at[c, st, s - 2]
        return pltpu.make_async_remote_copy(
            src_ref=src.at[:, part_cols(q)],
            dst_ref=chain.at[c, st, s - 1, :, part_cols(q)],
            send_sem=rs_send.at[c, st, s - 1, q],
            recv_sem=rs_recv.at[c, st, s - 1, q],
            device_id=(node, right if way > 0 else left),
            device_id_type=MESH,
        )

    def chip_part(c, p, h, q):
        return part[c, p, 0, h, :, part_cols(q)].astype(F32) + rsib[
            c, p, h, :, part_cols(q)
        ].astype(F32)

    def rs_start(c, which=turns):
        for q in range(PARTS):
            for st in which:
                way, h, hops = streams[st]
                chain_start[c, st, :, part_cols(q)] = chip_part(c, pos(way * hops), h, q).astype(BF16)
                rs(c, st, 1, q).start()

    def rs_step(c, s):
        for q in range(PARTS):
            for st in turns:
                way, h, hops = streams[st]
                if s < hops:
                    rs(c, st, s, q).wait_recv()
                    total = chain[c, st, s - 1, :, part_cols(q)].astype(F32)
                    total = total + chip_part(c, pos(way * (hops - s)), h, q)
                    chain[c, st, s - 1, :, part_cols(q)] = total.astype(BF16)
                    rs(c, st, s + 1, q).start()

    def rs_finish(c):
        sums = []
        for h in range(2):
            total = chip_sum(c, pos(0), h)
            for st in range(4):
                _, sh, hops = streams[st]
                if sh == h:
                    for q in range(PARTS):
                        rs(c, st, hops, q).wait_recv()
                    total = total + chain[c, st, hops - 1].astype(F32)
            sums.append(total)
        total = jnp.concatenate(sums, axis=0).astype(BF16)
        stack = [total[:, k * LANE : (k + 1) * LANE] for k in range(tiles)]
        stack.append(jnp.zeros(((SUB - tiles) * rows, LANE), BF16))
        back = dot_nn(pack_t[...], jnp.concatenate(stack, axis=0))
        tx2[c] = back.astype(BF16).reshape(nodes, SUB, LANE)
        rx2[c, node] = tx2[c, node]

    def back_to_node(c, lo, hi):
        to_node(tx2, rx2, back_send, back_recv, c, lo, hi)

    def combine(c, merge):
        all_of(tx2, rx2, back_send, back_recv, c).wait_recv()
        got = dot_nn(merge, rx2[c].reshape(slots, LANE))
        for k in range(tiles):
            out_ref[:, c * width + k * LANE : c * width + (k + 1) * LANE] = got[
                k * toks : (k + 1) * toks
            ].astype(BF16)

    constants = key_constants()
    all_of(tx, rx, out_send, out_recv, 0).wait_recv()
    with jax.named_scope("compact"):
        key = fill_key(constants)
        pack = one_hot(iota((packed, slots), 0) == key)
        compact(0, pack)
    ag_start(0)
    with jax.named_scope("unpack_matrix"):
        key_rows = fill_key_rows()
        for q in range(packed // LANE):
            pack_t[:, q * LANE : (q + 1) * LANE] = one_hot(
                key_rows == iota((slots, LANE), 1) + q * LANE
            )
    for s in range(1, C1_AFTER + 1):
        ag_step(0, s)
    all_of(tx, rx, out_send, out_recv, 1).wait_recv()
    with jax.named_scope("compact"):
        compact(1, pack)
    ag_start(1)
    for load in loads:
        load.wait()
    last = len(order) - 1

    def pair(s):
        return (0, 1) if s == half else (pos(s), pos(-s) + 1) if s else (last, last + 1)

    def hidden(s):
        p0, p1 = pair(s)
        for c in range(CHUNKS):
            sib_wait(c, range(p0, p1))
            project(c, p0, p1)
        activate(p0, p1)

    for s in range(1, half):
        if s + C1_AFTER <= half:
            ag_step(0, s + C1_AFTER)
        ag_step(1, s)
        hidden(s - 1)
    expand(0, 3, last + 1)
    if C1_AFTER == 0:
        ag_step(0, half)
    ag_step(1, half)
    hidden(half - 1)
    expand(0, 1, 3)
    for p in range(1, 3):
        psib(0, p).wait_recv()
    rs_start(0, (1, 2))
    hidden(half)
    expand(0, 0, 1)
    for p in (0, *range(3, last + 1)):
        psib(0, p).wait_recv()
    rs_start(0, (0, 3))
    expand(1, 0, last + 1)
    for p in range(last + 1):
        psib(1, p).wait_recv()
    if RS_LAG == 0:
        rs_start(1)
    for s in range(1, half):
        rs_step(0, s)
        if s == RS_LAG:
            rs_start(1)
        if s > RS_LAG:
            rs_step(1, s - RS_LAG)
    rs_finish(0)
    cuts = [(nodes - 1) * i // (RS_LAG + 1) for i in range(RS_LAG + 2)]
    back_to_node(0, cuts[0], cuts[1])
    for i in range(RS_LAG):
        rs_step(1, half - RS_LAG + i)
        back_to_node(0, cuts[i + 1], cuts[i + 2])
    rs_finish(1)
    back_to_node(1, 0, nodes - 1)
    with jax.named_scope("merge_matrix"):
        spot = iota((LANE, nodes * SUB), 1)
        tok_row = one_hot(iota((LANE, toks), 0) % toks == iota((LANE, toks), 1))
        ids_rows = dot_nt(tok_row, idf).astype(jnp.int32)
        row_tile = iota((LANE, 1), 0) // toks
        hit = None
        for j in range(picks):
            same = spot == ids_rows[:, j : j + 1] * SUB + row_tile
            hit = same if hit is None else hit | same
        merge = one_hot(hit)
    for c in range(CHUNKS):
        combine(c, merge)

    for c in range(CHUNKS):
        all_of(tx, rx, out_send, out_recv, c).wait_send()
        all_of(tx2, rx2, back_send, back_recv, c).wait_send()
        for st in range(4):
            for s in range(1, streams[st][2] + 1):
                for q in range(PARTS):
                    ag(c, st, s, q).wait_send()
                    rs(c, st, s, q).wait_send()
        for p in range(last + 1):
            to_sibling(c, p).wait_send()
            psib(c, p).wait_send()


def layer(cfg, og, ids, rw, sg, su, wg, wu, wd):
    nodes, ring, toks, picks, tiles = cfg
    half = ring // 2
    rows = toks * picks
    width = tiles * LANE
    slots = nodes * SUB
    piece = rows // 2
    dma = pltpu.SemaphoreType.DMA
    sg = sg.reshape(2 * ring, rows, LANE)
    su = su.reshape(2 * ring, rows, LANE)
    in_vmem = pl.BlockSpec(memory_space=pltpu.VMEM)
    return pl.pallas_call(
        functools.partial(kernel, cfg),
        out_shape=jax.ShapeDtypeStruct(og.shape, BF16),
        in_specs=[pl.BlockSpec(memory_space=pltpu.HBM)] * 8,
        out_specs=in_vmem,
        scratch_shapes=[
            pltpu.VMEM(og.shape, BF16),
            pltpu.VMEM(ids.shape[::-1], jnp.int32),
            pltpu.VMEM(rw.shape, BF16),
            pltpu.VMEM(sg.shape, BF16),
            pltpu.VMEM(su.shape, BF16),
            pltpu.VMEM(wd.shape, BF16),
            pltpu.VMEM((wg.shape[0], 2 * LANE), BF16),
            pltpu.VMEM((CHUNKS, nodes, SUB, LANE), BF16),
            pltpu.VMEM((CHUNKS, nodes, SUB, LANE), BF16),
            pltpu.VMEM((CHUNKS, nodes, SUB, LANE), BF16),
            pltpu.VMEM((CHUNKS, nodes, SUB, LANE), BF16),
            pltpu.VMEM((ring, 2, 2, piece, width + LANE), BF16),
            pltpu.VMEM((ring, 2, 2, piece, width), BF16),
            pltpu.VMEM((slots, SUB * rows), BF16),
            pltpu.VMEM((ring * 2 * rows, LANE), F32),
            pltpu.VMEM((ring, 2, rows, 2 * LANE), BF16),
            pltpu.VMEM((CHUNKS, ring, 2, 2, piece, width), BF16),
            pltpu.VMEM((CHUNKS, ring, 2, piece, width), BF16),
            pltpu.VMEM((CHUNKS, 4, piece, width), BF16),
            pltpu.VMEM((CHUNKS, 4, half, piece, width), BF16),
            dma((8,)),
            dma((CHUNKS,)),
            dma((CHUNKS,)),
            dma((CHUNKS,)),
            dma((CHUNKS,)),
            dma((CHUNKS, 4, half, PARTS)),
            dma((CHUNKS, 4, half, PARTS)),
            dma((CHUNKS, ring)),
            dma((CHUNKS, ring)),
            dma((CHUNKS, ring)),
            dma((CHUNKS, ring)),
            dma((CHUNKS, 4, half, PARTS)),
            dma((CHUNKS, 4, half, PARTS)),
        ],
        compiler_params=pltpu.CompilerParams(
            collective_id=0, has_side_effects=True, vmem_limit_bytes=VMEM_BYTES
        ),
    )(og, ids.T, rw, sg, su, wg, wu, wd)


def solution(mesh):
    nodes = mesh.shape["node"]
    ring = mesh.shape["local"] // 2

    def shards(og, ids, rw, sg, su, wg, wu, wd):
        toks, model = og.shape
        cfg = (nodes, ring, toks, ids.shape[1], model // (CHUNKS * LANE))
        return layer(cfg, og, ids, rw, sg, su, wg, wu, wd)

    return jax.shard_map(
        shards,
        mesh=mesh,
        in_specs=(
            P(("node", "local"), None),
            P(("node", "local"), None),
            P(("node", "local"), None),
            P("node", "local"),
            P("node", "local"),
            P(None, ("node", "local")),
            P(None, ("node", "local")),
            P(("node", "local"), None),
        ),
        out_specs=P(("node", "local"), None),
        check_vma=False,
    )
```

```python
import functools
import math

import jax
import jax.numpy as jnp
from jax import lax
from jax.experimental import pallas as pl
from jax.experimental.pallas import tpu as pltpu
from jax.sharding import PartitionSpec as P

MESH = pl.DeviceIdType.MESH
F32 = jnp.float32
BF16 = jnp.bfloat16
LANE = 128
SUB = 16
CHUNKS = 2
PARTS = 1
C1_AFTER = 0
RS_LAG = 2
VMEM_BYTES = 63 * 1024 * 1024


def iota(shape, dim):
    return lax.broadcasted_iota(jnp.int32, shape, dim)


def one_hot(cond):
    return jnp.where(cond, 1.0, 0.0).astype(BF16)


def dot_nn(a, b):
    return lax.dot_general(a, b, (((1,), (0,)), ((), ())), preferred_element_type=F32)


def dot_nt(a, b):
    return lax.dot_general(a, b, (((1,), (1,)), ((), ())), preferred_element_type=F32)


def kernel(
    cfg,
    og_hbm,
    ids_hbm,
    rw_hbm,
    sg_hbm,
    su_hbm,
    wg_hbm,
    wu_hbm,
    wd_hbm,
    out_ref,
    og_ref,
    ids_ref,
    rw_ref,
    sg,
    su,
    wd,
    wgu,
    tx,
    rx,
    tx2,
    rx2,
    x0,
    x1,
    pack_t,
    hacc,
    hid,
    part,
    rsib,
    chain_start,
    chain,
    load_sem,
    out_send,
    out_recv,
    back_send,
    back_recv,
    ag_send,
    ag_recv,
    sib_send,
    sib_recv,
    psib_send,
    psib_recv,
    rs_send,
    rs_recv,
):
    nodes, ring, toks, picks, tiles = cfg
    half = ring // 2
    rows = toks * picks
    slots = nodes * SUB
    packed = SUB * rows
    width = tiles * LANE
    xs = (x0, x1)

    node = lax.axis_index("node")
    local = lax.axis_index("local")
    y = local // 2
    core = local % 2
    right = ((y + 1) % ring) * 2 + core
    left = ((y + ring - 1) % ring) * 2 + core
    sibling = y * 2 + (1 - core)

    order = [half]
    for s in range(half - 1, 0, -1):
        order += [s, -s]
    order.append(0)

    def pos(d):
        return order.index(half if d == -half else d)

    streams = ((1, 0, half), (1, 1, half - 1), (-1, 0, half - 1), (-1, 1, half))

    firsts = [
        pltpu.make_async_copy(ids_hbm, ids_ref, load_sem.at[5]),
        pltpu.make_async_copy(rw_hbm, rw_ref, load_sem.at[6]),
        pltpu.make_async_copy(og_hbm, og_ref, load_sem.at[7]),
    ]
    for first in firsts:
        first.start()

    barrier = pltpu.get_barrier_semaphore()

    side = math.isqrt(nodes)

    def farthest(j):
        return side // 2 + ((j + 1) // 2) * (1 - 2 * (j % 2))

    def peer_at(i):
        first = (node // side + farthest(i // side) + side) % side
        second = (node % side + farthest(i % side) + side) % side
        return first * side + second

    def greet(i, carry):
        peer = peer_at(i)
        pl.semaphore_signal(barrier, inc=1, device_id=(peer, local), device_id_type=MESH)
        return carry

    lax.fori_loop(0, nodes - 1, greet, 0)
    for who in (right, left, sibling):
        pl.semaphore_signal(barrier, inc=1, device_id=(node, who), device_id_type=MESH)

    loads = [
        pltpu.make_async_copy(wd_hbm, wd, load_sem.at[0]),
        pltpu.make_async_copy(sg_hbm, sg, load_sem.at[1]),
        pltpu.make_async_copy(su_hbm, su, load_sem.at[2]),
        pltpu.make_async_copy(wg_hbm, wgu.at[:, pl.ds(0, LANE)], load_sem.at[3]),
        pltpu.make_async_copy(wu_hbm, wgu.at[:, pl.ds(LANE, LANE)], load_sem.at[4]),
    ]
    for load in loads:
        load.start()

    for first in firsts:
        first.wait()
    with jax.named_scope("fill_slots"):
        idf = ids_ref[...].astype(F32).astype(BF16)
        gates = rw_ref[...].astype(F32)
        lane8 = iota((toks, LANE), 1)
        repeat = one_hot(lane8 % toks == iota((toks, LANE), 0))
        ids_lanes = dot_nn(idf, repeat).astype(jnp.int32)
        ids_lane = [ids_lanes[j : j + 1] for j in range(picks)]
        lane1 = iota((1, LANE), 1)
        slot_row = iota((slots, LANE), 0)
        hit = None
        for j in range(picks):
            key = ids_lane[j] * SUB + lane1 // toks
            same = slot_row == key
            hit = same if hit is None else hit | same
        spread = one_hot(hit)
        pick_key = jnp.full((1, LANE), -1, jnp.int32)
        for j in range(picks):
            mine = ((lane1 // toks) % picks == j) & (lane1 < 2 * rows)
            pick_key = jnp.where(mine, ids_lane[j] * SUB + (SUB - 2) + lane1 // rows, pick_key)
        spread_meta = one_hot(slot_row == pick_key)
        meta = [
            jnp.where(
                lane8 < LANE // 2,
                gates[:, 2 * j : 2 * j + 1],
                gates[:, 2 * j + 1 : 2 * j + 2],
            )
            for j in range(picks)
        ]
        meta = jnp.concatenate(
            meta + [jnp.ones((rows, LANE), F32), jnp.zeros((LANE - 2 * rows, LANE), F32)], axis=0
        ).astype(BF16)
        meta_slots = dot_nn(spread_meta, meta)
        grads = og_ref[...].astype(F32)
        for c in range(CHUNKS):
            stack = [
                grads[:, c * width + k * LANE : c * width + (k + 1) * LANE] for k in range(tiles)
            ]
            stack.append(jnp.zeros((LANE - tiles * toks, LANE), F32))
            block = dot_nn(spread, jnp.concatenate(stack, axis=0).astype(BF16))
            if c == 0:
                block = block + meta_slots
            tx[c] = block.astype(BF16).reshape(nodes, SUB, LANE)
            rx[c, node] = tx[c, node]

    pl.semaphore_wait(barrier, nodes - 1 + 3)

    def to_node(src, dst, send_sem, recv_sem, c, lo=0, hi=nodes - 1):
        def go(i, carry):
            peer = peer_at(i)
            pltpu.make_async_remote_copy(
                src_ref=src.at[c, peer],
                dst_ref=dst.at[c, node],
                send_sem=send_sem.at[c],
                recv_sem=recv_sem.at[c],
                device_id=(peer, local),
                device_id_type=MESH,
            ).start()
            return carry

        lax.fori_loop(lo, hi, go, 0)

    def all_of(src, dst, send_sem, recv_sem, c):
        return pltpu.make_async_remote_copy(
            src_ref=src.at[c, pl.ds(0, nodes - 1)],
            dst_ref=dst.at[c, pl.ds(0, nodes - 1)],
            send_sem=send_sem.at[c],
            recv_sem=recv_sem.at[c],
            device_id=(node, sibling),
            device_id_type=MESH,
        )

    to_node(tx, rx, out_send, out_recv, 0)
    to_node(tx, rx, out_send, out_recv, 1)

    def cols(c, q):
        lo = q * (tiles // PARTS) * LANE
        hi = (q + 1) * (tiles // PARTS) * LANE
        if q == PARTS - 1:
            hi = width + (LANE if c == 0 else 0)
        return pl.ds(lo, hi - lo)

    def ag(c, st, s, q):
        way, h, _ = streams[st]
        return pltpu.make_async_remote_copy(
            src_ref=xs[c].at[pos(-way * (s - 1)), 0, h, :, cols(c, q)],
            dst_ref=xs[c].at[pos(-way * s), 0, h, :, cols(c, q)],
            send_sem=ag_send.at[c, st, s - 1, q],
            recv_sem=ag_recv.at[c, st, s - 1, q],
            device_id=(node, right if way > 0 else left),
            device_id_type=MESH,
        )

    def to_sibling(c, p):
        return pltpu.make_async_remote_copy(
            src_ref=xs[c].at[p, 0],
            dst_ref=xs[c].at[p, 1],
            send_sem=sib_send.at[c, p],
            recv_sem=sib_recv.at[c, p],
            device_id=(node, sibling),
            device_id_type=MESH,
        )

    turns = (0, 3, 1, 2)

    def ag_start(c):
        for q in range(PARTS):
            for st in turns:
                ag(c, st, 1, q).start()
        to_sibling(c, pos(0)).start()

    def ag_step(c, s):
        for q in range(PARTS):
            for st in turns:
                way, h, hops = streams[st]
                if s <= hops:
                    ag(c, st, s, q).wait_recv()
                    if s < hops:
                        ag(c, st, s + 1, q).start()

        for p in sorted({pos(s), pos(-s)}):
            to_sibling(c, p).start()

    def sib_wait(c, ps):
        for p in ps:
            to_sibling(c, p).wait_recv()

    def key_constants():
        first = one_hot(iota((SUB, LANE), 1) == 0)
        owner = one_hot(iota((slots, LANE), 0) // SUB == iota((slots, LANE), 1))
        below = one_hot(iota((LANE, slots), 0) <= iota((LANE, slots), 1) // SUB)
        equal = one_hot(iota((LANE, slots), 0) == iota((LANE, slots), 1) // SUB)
        return first, owner, below, equal

    def fill_key(constants):
        first, owner, below, equal = constants
        flat = rx[0].reshape(slots, LANE)
        lane_s = iota((SUB, slots), 1)
        flag = jnp.where(lane_s % SUB == SUB - 1, dot_nt(first, flat), 0.0).astype(BF16)
        by_node = dot_nn(flag, owner).astype(BF16)
        count = dot_nn(by_node, below)[0:1]
        filled = dot_nn(by_node, equal)[0:1]
        lane = iota((1, slots), 1)
        key = (lane % SUB) * rows + count.astype(jnp.int32) - 1
        return jnp.where(filled > 0.5, key, -1)

    def fill_key_rows():
        flat = rx[0].reshape(slots, LANE)
        take = one_hot(iota((LANE, slots), 1) == iota((LANE, slots), 0) * SUB + SUB - 1)
        by_node = dot_nn(take, flat).astype(BF16)
        below = one_hot(iota((slots, LANE), 1) <= iota((slots, LANE), 0) // SUB)
        equal = one_hot(iota((slots, LANE), 1) == iota((slots, LANE), 0) // SUB)
        count = dot_nn(below, by_node)
        filled = dot_nn(equal, by_node)
        key = (iota((slots, LANE), 0) % SUB) * rows + count.astype(jnp.int32) - 1
        return jnp.where(filled > 0.5, key, -1)

    def compact(c, pack):
        got = dot_nn(pack, rx[c].reshape(slots, LANE)).astype(BF16)
        for k in range(tiles + (1 if c == 0 else 0)):
            src = k if k < tiles else SUB - 2
            xs[c][pos(0), 0, :, :, k * LANE : (k + 1) * LANE] = got[
                src * rows : (src + 1) * rows
            ].reshape(2, rows // 2, LANE)

    def project(c, p0, p1):
        lhs = xs[c][p0:p1, :, :, :, 0:width].reshape((p1 - p0) * 2 * rows, width)
        value = dot_nt(lhs, wd[:, c * width : (c + 1) * width])
        span = pl.ds(p0 * 2 * rows, (p1 - p0) * 2 * rows)
        if c == 0:
            hacc[span, :] = value
        else:
            hacc[span, :] = hacc[span, :] + value

    own_slot = local // (ring * 2 // 2)

    def activate(p0, p1):
        for p in range(p0, p1):
            for who in range(2):
                src_core = core if who == 0 else 1 - core
                src = ((y + order[p] + ring) % ring) * 2 + src_core
                a = sg[src].astype(F32)
                b = su[src].astype(F32)
                g = xs[0][p, who, :, :, width : width + LANE].reshape(rows, LANE).astype(F32)
                gate = jnp.where(own_slot == 0, g[:, 0:1], g[:, LANE // 2 : LANE // 2 + 1])
                base = (p * 2 + who) * rows
                grad = gate * hacc[base : base + rows, :]
                sig = 1.0 / (1.0 + jnp.exp(-a))
                hid[p, who, :, 0:LANE] = (grad * b * sig * (1.0 + a * (1.0 - sig))).astype(BF16)
                hid[p, who, :, LANE : 2 * LANE] = (grad * a * sig).astype(BF16)

    def psib(c, p):
        return pltpu.make_async_remote_copy(
            src_ref=part.at[c, p, 1],
            dst_ref=rsib.at[c, p],
            send_sem=psib_send.at[c, p],
            recv_sem=psib_recv.at[c, p],
            device_id=(node, sibling),
            device_id_type=MESH,
        )

    step_cols = 2 * LANE if width % (2 * LANE) == 0 else LANE

    def expand(c, p0, p1):
        lhs = hid[p0:p1].reshape((p1 - p0) * 2 * rows, 2 * LANE)
        for n in range(0, width, step_cols):
            value = dot_nt(lhs, wgu[c * width + n : c * width + n + step_cols, :])
            part[c, p0:p1, :, :, :, n : n + step_cols] = value.astype(BF16).reshape(
                p1 - p0, 2, 2, rows // 2, step_cols
            )
        for p in range(p0, p1):
            psib(c, p).start()

    def chip_sum(c, p, h):
        return part[c, p, 0, h].astype(F32) + rsib[c, p, h].astype(F32)

    def part_cols(q):
        return pl.ds(q * (width // PARTS), width // PARTS)

    def rs(c, st, s, q):
        way = streams[st][0]
        src = chain_start.at[c, st] if s == 1 else chain.at[c, st, s - 2]
        return pltpu.make_async_remote_copy(
            src_ref=src.at[:, part_cols(q)],
            dst_ref=chain.at[c, st, s - 1, :, part_cols(q)],
            send_sem=rs_send.at[c, st, s - 1, q],
            recv_sem=rs_recv.at[c, st, s - 1, q],
            device_id=(node, right if way > 0 else left),
            device_id_type=MESH,
        )

    def chip_part(c, p, h, q):
        return part[c, p, 0, h, :, part_cols(q)].astype(F32) + rsib[
            c, p, h, :, part_cols(q)
        ].astype(F32)

    def rs_start(c, which=turns):
        for q in range(PARTS):
            for st in which:
                way, h, hops = streams[st]
                chain_start[c, st, :, part_cols(q)] = chip_part(c, pos(way * hops), h, q).astype(BF16)
                rs(c, st, 1, q).start()

    def rs_step(c, s):
        for q in range(PARTS):
            for st in turns:
                way, h, hops = streams[st]
                if s < hops:
                    rs(c, st, s, q).wait_recv()
                    total = chain[c, st, s - 1, :, part_cols(q)].astype(F32)
                    total = total + chip_part(c, pos(way * (hops - s)), h, q)
                    chain[c, st, s - 1, :, part_cols(q)] = total.astype(BF16)
                    rs(c, st, s + 1, q).start()

    def rs_finish(c):
        sums = []
        for h in range(2):
            total = chip_sum(c, pos(0), h)
            for st in range(4):
                _, sh, hops = streams[st]
                if sh == h:
                    for q in range(PARTS):
                        rs(c, st, hops, q).wait_recv()
                    total = total + chain[c, st, hops - 1].astype(F32)
            sums.append(total)
        total = jnp.concatenate(sums, axis=0).astype(BF16)
        stack = [total[:, k * LANE : (k + 1) * LANE] for k in range(tiles)]
        stack.append(jnp.zeros(((SUB - tiles) * rows, LANE), BF16))
        back = dot_nn(pack_t[...], jnp.concatenate(stack, axis=0))
        tx2[c] = back.astype(BF16).reshape(nodes, SUB, LANE)
        rx2[c, node] = tx2[c, node]

    def back_to_node(c, lo, hi):
        to_node(tx2, rx2, back_send, back_recv, c, lo, hi)

    def combine(c, merge):
        all_of(tx2, rx2, back_send, back_recv, c).wait_recv()
        got = dot_nn(merge, rx2[c].reshape(slots, LANE))
        for k in range(tiles):
            out_ref[:, c * width + k * LANE : c * width + (k + 1) * LANE] = got[
                k * toks : (k + 1) * toks
            ].astype(BF16)

    constants = key_constants()
    all_of(tx, rx, out_send, out_recv, 0).wait_recv()
    with jax.named_scope("compact"):
        key = fill_key(constants)
        pack = one_hot(iota((packed, slots), 0) == key)
        compact(0, pack)
    ag_start(0)
    with jax.named_scope("unpack_matrix"):
        key_rows = fill_key_rows()
        for q in range(packed // LANE):
            pack_t[:, q * LANE : (q + 1) * LANE] = one_hot(
                key_rows == iota((slots, LANE), 1) + q * LANE
            )
    for s in range(1, C1_AFTER + 1):
        ag_step(0, s)
    all_of(tx, rx, out_send, out_recv, 1).wait_recv()
    with jax.named_scope("compact"):
        compact(1, pack)
    ag_start(1)
    for load in loads:
        load.wait()
    last = len(order) - 1

    def pair(s):
        return (0, 1) if s == half else (pos(s), pos(-s) + 1) if s else (last, last + 1)

    def hidden(s):
        p0, p1 = pair(s)
        for c in range(CHUNKS):
            sib_wait(c, range(p0, p1))
            project(c, p0, p1)
        activate(p0, p1)

    for s in range(1, half):
        if s + C1_AFTER <= half:
            ag_step(0, s + C1_AFTER)
        ag_step(1, s)
        hidden(s - 1)
    for c in range(CHUNKS):
        expand(c, 3, last + 1)
    if C1_AFTER == 0:
        ag_step(0, half)
    ag_step(1, half)
    hidden(half - 1)
    expand(0, 1, 3)
    for p in range(1, 3):
        psib(0, p).wait_recv()
    rs_start(0, (1, 2))
    hidden(half)
    expand(0, 0, 1)
    for p in (0, *range(3, last + 1)):
        psib(0, p).wait_recv()
    rs_start(0, (0, 3))
    expand(1, 0, 3)
    for s in range(1, half):
        rs_step(0, s)
        if s == RS_LAG:
            for p in range(last + 1):
                psib(1, p).wait_recv()
            rs_start(1)
        if s > RS_LAG:
            rs_step(1, s - RS_LAG)
    rs_finish(0)
    cuts = [(nodes - 1) * i // (RS_LAG + 1) for i in range(RS_LAG + 2)]
    back_to_node(0, cuts[0], cuts[1])
    for i in range(RS_LAG):
        rs_step(1, half - RS_LAG + i)
        back_to_node(0, cuts[i + 1], cuts[i + 2])
    rs_finish(1)
    back_to_node(1, 0, nodes - 1)
    with jax.named_scope("merge_matrix"):
        spot = iota((LANE, nodes * SUB), 1)
        tok_row = one_hot(iota((LANE, toks), 0) % toks == iota((LANE, toks), 1))
        ids_rows = dot_nt(tok_row, idf).astype(jnp.int32)
        row_tile = iota((LANE, 1), 0) // toks
        hit = None
        for j in range(picks):
            same = spot == ids_rows[:, j : j + 1] * SUB + row_tile
            hit = same if hit is None else hit | same
        merge = one_hot(hit)
    for c in range(CHUNKS):
        combine(c, merge)

    for c in range(CHUNKS):
        all_of(tx, rx, out_send, out_recv, c).wait_send()
        all_of(tx2, rx2, back_send, back_recv, c).wait_send()
        for st in range(4):
            for s in range(1, streams[st][2] + 1):
                for q in range(PARTS):
                    ag(c, st, s, q).wait_send()
                    rs(c, st, s, q).wait_send()
        for p in range(last + 1):
            to_sibling(c, p).wait_send()
            psib(c, p).wait_send()


def layer(cfg, og, ids, rw, sg, su, wg, wu, wd):
    nodes, ring, toks, picks, tiles = cfg
    half = ring // 2
    rows = toks * picks
    width = tiles * LANE
    slots = nodes * SUB
    piece = rows // 2
    dma = pltpu.SemaphoreType.DMA
    sg = sg.reshape(2 * ring, rows, LANE)
    su = su.reshape(2 * ring, rows, LANE)
    in_vmem = pl.BlockSpec(memory_space=pltpu.VMEM)
    return pl.pallas_call(
        functools.partial(kernel, cfg),
        out_shape=jax.ShapeDtypeStruct(og.shape, BF16),
        in_specs=[pl.BlockSpec(memory_space=pltpu.HBM)] * 8,
        out_specs=in_vmem,
        scratch_shapes=[
            pltpu.VMEM(og.shape, BF16),
            pltpu.VMEM(ids.shape[::-1], jnp.int32),
            pltpu.VMEM(rw.shape, BF16),
            pltpu.VMEM(sg.shape, BF16),
            pltpu.VMEM(su.shape, BF16),
            pltpu.VMEM(wd.shape, BF16),
            pltpu.VMEM((wg.shape[0], 2 * LANE), BF16),
            pltpu.VMEM((CHUNKS, nodes, SUB, LANE), BF16),
            pltpu.VMEM((CHUNKS, nodes, SUB, LANE), BF16),
            pltpu.VMEM((CHUNKS, nodes, SUB, LANE), BF16),
            pltpu.VMEM((CHUNKS, nodes, SUB, LANE), BF16),
            pltpu.VMEM((ring, 2, 2, piece, width + LANE), BF16),
            pltpu.VMEM((ring, 2, 2, piece, width), BF16),
            pltpu.VMEM((slots, SUB * rows), BF16),
            pltpu.VMEM((ring * 2 * rows, LANE), F32),
            pltpu.VMEM((ring, 2, rows, 2 * LANE), BF16),
            pltpu.VMEM((CHUNKS, ring, 2, 2, piece, width), BF16),
            pltpu.VMEM((CHUNKS, ring, 2, piece, width), BF16),
            pltpu.VMEM((CHUNKS, 4, piece, width), BF16),
            pltpu.VMEM((CHUNKS, 4, half, piece, width), BF16),
            dma((8,)),
            dma((CHUNKS,)),
            dma((CHUNKS,)),
            dma((CHUNKS,)),
            dma((CHUNKS,)),
            dma((CHUNKS, 4, half, PARTS)),
            dma((CHUNKS, 4, half, PARTS)),
            dma((CHUNKS, ring)),
            dma((CHUNKS, ring)),
            dma((CHUNKS, ring)),
            dma((CHUNKS, ring)),
            dma((CHUNKS, 4, half, PARTS)),
            dma((CHUNKS, 4, half, PARTS)),
        ],
        compiler_params=pltpu.CompilerParams(
            collective_id=0, has_side_effects=True, vmem_limit_bytes=VMEM_BYTES
        ),
    )(og, ids.T, rw, sg, su, wg, wu, wd)


def solution(mesh):
    nodes = mesh.shape["node"]
    ring = mesh.shape["local"] // 2

    def shards(og, ids, rw, sg, su, wg, wu, wd):
        toks, model = og.shape
        cfg = (nodes, ring, toks, ids.shape[1], model // (CHUNKS * LANE))
        return layer(cfg, og, ids, rw, sg, su, wg, wu, wd)

    return jax.shard_map(
        shards,
        mesh=mesh,
        in_specs=(
            P(("node", "local"), None),
            P(("node", "local"), None),
            P(("node", "local"), None),
            P("node", "local"),
            P("node", "local"),
            P(None, ("node", "local")),
            P(None, ("node", "local")),
            P(("node", "local"), None),
        ),
        out_specs=P(("node", "local"), None),
        check_vma=False,
    )
```
